32 devices in a mesh: parts: 2 (over x), blk: 16 (over z, y, core).
Axes of the slice: x: 2, y: 2, z: 4, core: 2. Of those that a mesh axis runs over, the one named last changes fastest.
Arguments:
- half_blocks: bfloat16 [4096, 24000], P(('parts', 'blk')), parts along dimension 0, may hold values from -6 to 6
Outputs:
- exchange_band: float32 [4096, 640], P(('parts', 'blk')), parts along dimension 0
The draws below stay inside these ranges and needn't reach their ends.
There are 2 independent parts, one for each index of `parts`. The reference program is written for one: setup_inputs(seed, part) draws one part's arguments, and reference() takes and returns one part's arrays. A program takes and returns all parts, laid end to end along the dimension named above; each array names one. Nothing has to cross between parts.
All inputs are finite; a program needn't handle non-finite values.
Results may differ from the reference program's by a relative error of at most 0.0003.
Values may be sent and summed in bfloat16 or wider, within the bound.
A program may use at most 64 MiB of HBM per device.

```python
import math
import jax
import jax.numpy as jnp
from jax import lax

MB = 128
AUXB = 16
OCC = 1500
BAND = 5
NBF = 2048


def block_scale(key, shape, cuts, low, largest):
    gain, own = 1.0, jax.random.fold_in(key, 6)
    for dim, shards_of in cuts:
        steps = jnp.exp(jax.random.uniform(jax.random.fold_in(own, dim), (shards_of,), jnp.float32, low / len(cuts), largest / len(cuts)))
        gain = gain * jnp.repeat(steps, shape[dim] // shards_of).reshape([-1 if axis == dim else 1 for axis in range(len(shape))])
    return gain


def centred(key, extent, deviation, limit, split=(), held_as=jnp.bfloat16):
    values = deviation * jax.random.normal(key, extent, jnp.float32)
    if split:
        values = values * block_scale(key, extent, split, -0.22, 0.18)
    return jnp.clip(values, -limit, limit).astype(held_as)


def setup_inputs(seed: int = 0, part: int = 0) -> dict:
    arg_keys = jax.random.split(jax.random.key(seed), 2)
    part_keys = jax.random.split(jax.random.fold_in(arg_keys[1], part), 2)
    return {
        "half_blocks": centred(part_keys[0], (NBF, AUXB * OCC), 1.0, 6.0, ((0, 16),)),
    }


def reference(half_blocks):
    count = NBF // MB
    blocks = half_blocks.reshape(count, MB, AUXB * OCC)
    factor = 1.0 / math.sqrt(AUXB * OCC)

    def block_row(index):
        mine = lax.dynamic_index_in_dim(blocks, index, 0, keepdims=False)
        tiles = []
        for offset in range(BAND):
            other_index = jnp.mod(index + offset - 2, count).astype(jnp.int32)
            other = lax.dynamic_index_in_dim(blocks, other_index, 0, keepdims=False)
            product = lax.dot_general(mine, other, (((1,), (1,)), ((), ())), preferred_element_type=jnp.float32)
            tiles.append(product * factor)
        return jnp.concatenate(tiles, axis=1)
    rows = lax.map(block_row, jnp.arange(count, dtype=jnp.int32))
    return rows.reshape(NBF, BAND * MB)
```

```python
import functools
import math

import jax
import jax.numpy as jnp
from jax import lax
from jax.experimental import pallas as pl
from jax.experimental.pallas import tpu as pltpu
from jax.sharding import PartitionSpec as P

TILE = 128
PIECES = 15
F32 = jnp.float32


def gram(left, right):
    return lax.dot_general(left, right, (((0,), (0,)), ((), ())), preferred_element_type=F32)


def kernel(
    n, a_ref, out_ref, mine, cols, other, spare, acc, peer, ymsg, lohi, zout, cross, crossrecv, diag,
    load_sem, send_sem, y_sem, z_sem, sib_sem, tail_send, tail_recv,
):
    depth = a_ref.shape[0]
    quarter = depth // 4
    size = quarter // PIECES
    rows = n // 4
    me = lax.axis_index("blk")
    k = lax.rem(me, 2)
    y = lax.rem(me // 2, 2)
    r = me // 4
    to_row = lax.rem(r + 2 * y - 1 + rows, rows)
    from_row = lax.rem(r - 2 * y + 1 + rows, rows)

    def dev(row, half, core):
        return row * 4 + half * 2 + core

    sibling = dev(r, y, 1 - k)
    barrier = pltpu.get_barrier_semaphore()
    partners = [sibling]
    for core in range(2):
        partners += [dev(r, 1 - y, core), dev(to_row, y, core), dev(from_row, y, core)]
    for partner in partners:
        pl.semaphore_signal(barrier, inc=1, device_id={"blk": partner})

    def span(half, core, start, count):
        return pl.ds(pl.multiple_of((half * 2 + core) * quarter + start, 16), count)

    load_all = pltpu.make_async_copy(a_ref, mine, load_sem.at[0])
    load_all.start()
    load_part = pltpu.make_async_copy(
        a_ref.at[span(y, k, 0, quarter)], cols.at[2 * y + k], load_sem.at[1]
    )
    load_part.start()
    acc[...] = jnp.zeros_like(acc)
    peer[0, 3] = jnp.zeros((TILE, TILE), F32)
    peer[1, 0] = jnp.zeros((TILE, TILE), F32)
    cross[...] = jnp.zeros_like(cross)
    diag[...] = jnp.zeros_like(diag)
    pl.semaphore_wait(barrier, len(partners))

    def y_copy(core, c, count, slot, sem):
        start = pl.multiple_of(c * size, 16)
        return pltpu.make_async_remote_copy(
            src_ref=a_ref.at[span(1 - y, core, start, count)],
            dst_ref=other.at[slot, pl.ds(start, count)],
            send_sem=send_sem.at[core],
            recv_sem=sem,
            device_id={"blk": dev(r, 1 - y, core)},
        )

    def z_copy(core, c, count, slot, sem):
        start = pl.multiple_of(c * size, 16)
        return pltpu.make_async_remote_copy(
            src_ref=a_ref.at[span(y, core, start, count)],
            dst_ref=cols.at[2 * (1 - y) + slot, pl.ds(start, count)],
            send_sem=send_sem.at[2 + core],
            recv_sem=sem,
            device_id={"blk": dev(to_row, y, core)},
        )

    def send(c, carry):
        for core in range(2):
            z_copy(core, c, size, k, z_sem.at[k, c]).start()
            y_copy(core, c, size, k, y_sem.at[k, c]).start()
        return carry

    send(0, 0)
    sib_one = pltpu.make_async_remote_copy(
        src_ref=a_ref.at[span(y, 1 - k, 0, quarter)],
        dst_ref=cols.at[2 * y + k],
        send_sem=send_sem.at[4],
        recv_sem=sib_sem.at[0],
        device_id={"blk": sibling},
    )
    sib_one.start()
    sib_two = pltpu.make_async_remote_copy(
        src_ref=a_ref.at[span(1 - y, 1 - k, 0, quarter)],
        dst_ref=spare,
        send_sem=send_sem.at[5],
        recv_sem=sib_sem.at[1],
        device_id={"blk": sibling},
    )
    sib_two.start()
    lax.fori_loop(1, PIECES, send, 0)

    load_all.wait()
    load_part.wait()

    def diag_step(c, carry):
        part = mine[pl.ds(pl.multiple_of(c * size, 16), size), :]
        diag[...] += gram(part, part)
        return carry

    lax.fori_loop(0, 4 * PIECES, diag_step, 0)

    pltpu.make_async_remote_copy(
        src_ref=a_ref.at[span(y, 1 - k, 0, quarter)],
        dst_ref=cols.at[2 * y + 1 - k],
        send_sem=send_sem.at[4],
        recv_sem=sib_sem.at[0],
        device_id={"blk": sibling},
    ).wait_recv()
    sib_two.wait_recv()

    def cross_step(c, carry):
        start = pl.multiple_of(c * size, 16)
        cross[...] += gram(cols[2 * y + 1 - k, pl.ds(start, size), :], mine[span(y, k, start, size), :])
        cross[...] += gram(spare[pl.ds(start, size), :], mine[span(1 - y, k, start, size), :])
        return carry

    lax.fori_loop(0, PIECES, cross_step, 0)

    send_cross = pltpu.make_async_remote_copy(
        src_ref=cross,
        dst_ref=crossrecv,
        send_sem=tail_send.at[0],
        recv_sem=tail_recv.at[0],
        device_id={"blk": sibling},
    )
    send_cross.start()

    def main_step(c, carry):
        for core in range(2):
            z_copy(core, c, size, core, z_sem.at[core, c]).wait_recv()
            y_copy(core, c, size, core, y_sem.at[core, c]).wait_recv()
        part = pl.ds(pl.multiple_of(c * size, 16), size)
        left = jnp.concatenate([other[0, part, :], other[1, part, :]], axis=1)
        right = jnp.concatenate([cols[t, part, :] for t in range(4)], axis=1)
        product = gram(left, right)
        for u in range(2):
            for t in range(u, u + 3):
                acc[u, t] += product[u * TILE : (u + 1) * TILE, t * TILE : (t + 1) * TILE]
        return carry

    lax.fori_loop(0, PIECES, main_step, 0)

    swaps = []
    for u in range(2):
        swap = pltpu.make_async_remote_copy(
            src_ref=acc.at[u, pl.ds(u, 3)],
            dst_ref=peer.at[u, pl.ds(u, 3)],
            send_sem=tail_send.at[1 + u],
            recv_sem=tail_recv.at[1 + u],
            device_id={"blk": sibling},
        )
        swap.start()
        swaps.append(swap)
    for u in range(2):
        swaps[u].wait_recv()
        for t in range(u, u + 3):
            peer[u, t] += acc[u, t]
    send_y = pltpu.make_async_remote_copy(
        src_ref=peer.at[k, pl.ds(k, 3)],
        dst_ref=ymsg,
        send_sem=tail_send.at[3],
        recv_sem=tail_recv.at[3],
        device_id={"blk": dev(r, 1 - y, k)},
    )
    send_y.start()
    for u in range(2):
        zout[u] = peer[u, 2 * (1 - y) + k].T
    send_z = pltpu.make_async_remote_copy(
        src_ref=zout,
        dst_ref=lohi.at[y],
        send_sem=tail_send.at[4],
        recv_sem=tail_recv.at[4],
        device_id={"blk": dev(from_row, y, k)},
    )
    send_z.start()
    for u in range(2):
        lohi[1 - y, u] = peer[u, 2 * y + k].T
    send_cross.wait_recv()
    out_ref[:, 2 * TILE : 3 * TILE] = diag[...]
    near = cross[...].T + crossrecv[...]
    send_z.wait_recv()
    send_y.wait_recv()

    @pl.when(k == 0)
    def _():
        out_ref[:, 0:TILE] = ymsg[0] + lohi[0, 0]
        out_ref[:, TILE : 2 * TILE] = ymsg[1] + lohi[0, 1]
        out_ref[:, 3 * TILE : 4 * TILE] = near
        out_ref[:, 4 * TILE : 5 * TILE] = ymsg[2] + lohi[1, 0]

    @pl.when(k == 1)
    def _():
        out_ref[:, 0:TILE] = ymsg[0] + lohi[0, 1]
        out_ref[:, TILE : 2 * TILE] = near
        out_ref[:, 3 * TILE : 4 * TILE] = ymsg[1] + lohi[1, 0]
        out_ref[:, 4 * TILE : 5 * TILE] = ymsg[2] + lohi[1, 1]

    for core in range(2):
        for copy in (y_copy, z_copy):
            copy(core, 0, quarter, k, y_sem.at[k, 0]).wait_send()
    sib_one.wait_send()
    sib_two.wait_send()
    send_cross.wait_send()
    for swap in swaps:
        swap.wait_send()
    send_y.wait_send()
    send_z.wait_send()


def body(n, half_blocks):
    columns = half_blocks.T
    depth, tile = columns.shape
    quarter = depth // 4
    band = pl.pallas_call(
        functools.partial(kernel, n),
        out_shape=jax.ShapeDtypeStruct((tile, 5 * tile), F32),
        in_specs=[pl.BlockSpec(memory_space=pl.ANY)],
        out_specs=pl.BlockSpec(memory_space=pltpu.VMEM),
        scratch_shapes=[
            pltpu.VMEM((depth, tile), jnp.bfloat16),
            pltpu.VMEM((4, quarter, tile), jnp.bfloat16),
            pltpu.VMEM((2, quarter, tile), jnp.bfloat16),
            pltpu.VMEM((quarter, tile), jnp.bfloat16),
            pltpu.VMEM((2, 4, tile, tile), F32),
            pltpu.VMEM((2, 4, tile, tile), F32),
            pltpu.VMEM((3, tile, tile), F32),
            pltpu.VMEM((2, 2, tile, tile), F32),
            pltpu.VMEM((2, tile, tile), F32),
            pltpu.VMEM((tile, tile), F32),
            pltpu.VMEM((tile, tile), F32),
            pltpu.VMEM((tile, tile), F32),
            pltpu.SemaphoreType.DMA((2,)),
            pltpu.SemaphoreType.DMA((6,)),
            pltpu.SemaphoreType.DMA((2, PIECES)),
            pltpu.SemaphoreType.DMA((2, PIECES)),
            pltpu.SemaphoreType.DMA((2,)),
            pltpu.SemaphoreType.DMA((5,)),
            pltpu.SemaphoreType.DMA((5,)),
        ],
        compiler_params=pltpu.CompilerParams(
            collective_id=0, has_side_effects=True, vmem_limit_bytes=60 * 1024 * 1024
        ),
    )(columns)
    return band * (1.0 / math.sqrt(depth))


def solution(mesh):
    return jax.shard_map(
        functools.partial(body, mesh.shape["blk"]),
        mesh=mesh,
        in_specs=(P(("parts", "blk"), None),),
        out_specs=P(("parts", "blk"), None),
        check_vma=False,
    )
```

```python
import functools
import math

import jax
import jax.numpy as jnp
from jax import lax
from jax.experimental import pallas as pl
from jax.experimental.pallas import tpu as pltpu
from jax.sharding import PartitionSpec as P

TILE = 128
PIECES = 15
LEAD = 3
F32 = jnp.float32


def gram(left, right):
    return lax.dot_general(left, right, (((0,), (0,)), ((), ())), preferred_element_type=F32)


def kernel(
    n, a_ref, out_ref, mine, cols, other, spare, acc, peer, ymsg, lohi, zout, cross, crossrecv, diag,
    load_sem, send_sem, y_sem, z_sem, sib_sem, tail_send, tail_recv,
):
    depth = a_ref.shape[0]
    quarter = depth // 4
    size = quarter // PIECES
    rows = n // 4
    me = lax.axis_index("blk")
    k = lax.rem(me, 2)
    y = lax.rem(me // 2, 2)
    r = me // 4
    to_row = lax.rem(r + 2 * y - 1 + rows, rows)
    from_row = lax.rem(r - 2 * y + 1 + rows, rows)

    def dev(row, half, core):
        return row * 4 + half * 2 + core

    sibling = dev(r, y, 1 - k)
    barrier = pltpu.get_barrier_semaphore()
    partners = [sibling]
    for core in range(2):
        partners += [dev(r, 1 - y, core), dev(to_row, y, core), dev(from_row, y, core)]
    for partner in partners:
        pl.semaphore_signal(barrier, inc=1, device_id={"blk": partner})

    def span(half, core, start, count):
        return pl.ds(pl.multiple_of((half * 2 + core) * quarter + start, 16), count)

    load_all = pltpu.make_async_copy(a_ref, mine, load_sem.at[0])
    load_all.start()
    load_part = pltpu.make_async_copy(
        a_ref.at[span(y, k, 0, quarter)], cols.at[2 * y + k], load_sem.at[1]
    )
    load_part.start()
    acc[...] = jnp.zeros_like(acc)
    peer[0, 3] = jnp.zeros((TILE, TILE), F32)
    peer[1, 0] = jnp.zeros((TILE, TILE), F32)
    cross[...] = jnp.zeros_like(cross)
    diag[...] = jnp.zeros_like(diag)
    pl.semaphore_wait(barrier, len(partners))

    def y_copy(core, c, count, slot, sem):
        start = pl.multiple_of(c * size, 16)
        return pltpu.make_async_remote_copy(
            src_ref=a_ref.at[span(1 - y, core, start, count)],
            dst_ref=other.at[slot, pl.ds(start, count)],
            send_sem=send_sem.at[core],
            recv_sem=sem,
            device_id={"blk": dev(r, 1 - y, core)},
        )

    def z_copy(core, c, count, slot, sem):
        start = pl.multiple_of(c * size, 16)
        return pltpu.make_async_remote_copy(
            src_ref=a_ref.at[span(y, core, start, count)],
            dst_ref=cols.at[2 * (1 - y) + slot, pl.ds(start, count)],
            send_sem=send_sem.at[2 + core],
            recv_sem=sem,
            device_id={"blk": dev(to_row, y, core)},
        )

    def send(wave, c):
        @pl.when(k == lax.rem(y + wave, 2))
        def _():
            for core in range(2):
                z_copy(core, c, size, k, z_sem.at[k, c]).start()

        @pl.when(k != lax.rem(y + wave, 2))
        def _():
            for core in range(2):
                y_copy(core, c, size, k, y_sem.at[k, c]).start()

    def send_wave(wave, first):
        def step(c, carry):
            send(wave, c)
            return carry

        lax.fori_loop(first, PIECES, step, 0)

    send(0, 0)
    sib_one = pltpu.make_async_remote_copy(
        src_ref=a_ref.at[span(y, 1 - k, 0, quarter)],
        dst_ref=cols.at[2 * y + k],
        send_sem=send_sem.at[4],
        recv_sem=sib_sem.at[0],
        device_id={"blk": sibling},
    )
    sib_one.start()
    sib_two = pltpu.make_async_remote_copy(
        src_ref=a_ref.at[span(1 - y, 1 - k, 0, quarter)],
        dst_ref=spare,
        send_sem=send_sem.at[5],
        recv_sem=sib_sem.at[1],
        device_id={"blk": sibling},
    )
    sib_two.start()
    send_wave(0, 1)

    load_all.wait()
    load_part.wait()

    def diag_step(c, carry):
        part = mine[pl.ds(pl.multiple_of(c * size, 16), size), :]
        diag[...] += gram(part, part)
        return carry

    lax.fori_loop(0, 4 * PIECES, diag_step, 0)

    pltpu.make_async_remote_copy(
        src_ref=a_ref.at[span(y, 1 - k, 0, quarter)],
        dst_ref=cols.at[2 * y + 1 - k],
        send_sem=send_sem.at[4],
        recv_sem=sib_sem.at[0],
        device_id={"blk": sibling},
    ).wait_recv()
    sib_two.wait_recv()

    def cross_step(c, carry):
        start = pl.multiple_of(c * size, 16)
        cross[...] += gram(cols[2 * y + 1 - k, pl.ds(start, size), :], mine[span(y, k, start, size), :])
        cross[...] += gram(spare[pl.ds(start, size), :], mine[span(1 - y, k, start, size), :])
        return carry

    lax.fori_loop(0, PIECES, cross_step, 0)

    send_cross = pltpu.make_async_remote_copy(
        src_ref=cross,
        dst_ref=crossrecv,
        send_sem=tail_send.at[0],
        recv_sem=tail_recv.at[0],
        device_id={"blk": sibling},
    )
    send_cross.start()

    waves = (y, 1 - y)

    def arrive(u, c):
        z_copy(0, c, size, u, z_sem.at[u, c]).wait_recv()
        y_copy(0, c, size, u, y_sem.at[u, c]).wait_recv()

    def multiply(u, c):
        part = pl.ds(pl.multiple_of(c * size, 16), size)
        right = jnp.concatenate([cols[u + t, part, :] for t in range(3)], axis=1)
        product = gram(other[u, part, :], right)
        for t in range(3):
            acc[u, u + t] += product[:, t * TILE : (t + 1) * TILE]

    def steps(u, first, last):
        def step(c, carry):
            arrive(u, c)
            multiply(u, c)
            return carry

        lax.fori_loop(first, last, step, 0)

    def swap(wave):
        u = waves[wave]
        return pltpu.make_async_remote_copy(
            src_ref=acc.at[u, pl.ds(u, 3)],
            dst_ref=peer.at[u, pl.ds(u, 3)],
            send_sem=tail_send.at[1 + wave],
            recv_sem=tail_recv.at[1 + wave],
            device_id={"blk": sibling},
        )

    def add_swapped(wave):
        u = waves[wave]
        swap(wave).wait_recv()
        for t in range(3):
            peer[u, u + t] += acc[u, u + t]

    send_y = pltpu.make_async_remote_copy(
        src_ref=peer.at[k, pl.ds(k, 3)],
        dst_ref=ymsg,
        send_sem=tail_send.at[3],
        recv_sem=tail_recv.at[3],
        device_id={"blk": dev(r, 1 - y, k)},
    )

    def send_z(wave):
        return pltpu.make_async_remote_copy(
            src_ref=zout.at[wave],
            dst_ref=lohi.at[y, waves[wave]],
            send_sem=tail_send.at[4 + wave],
            recv_sem=tail_recv.at[4 + wave],
            device_id={"blk": dev(from_row, y, k)},
        )

    def turn_z(wave):
        zout[wave] = peer[waves[wave], 2 * (1 - y) + k].T

    def turn_own(wave):
        u = waves[wave]
        lohi[1 - y, u] = peer[u, 2 * y + k].T

    steps(waves[0], 0, PIECES - LEAD)
    send_wave(1, 0)
    steps(waves[0], PIECES - LEAD, PIECES)
    swap(0).start()
    steps(waves[1], 0, PIECES - LEAD)
    add_swapped(0)
    turn_z(0)
    turn_own(0)
    steps(waves[1], PIECES - LEAD, PIECES - 1)
    arrive(waves[1], PIECES - 1)

    @pl.when(k == y)
    def _():
        send_y.start()

    @pl.when(k == y)
    def _():
        send_z(0).start()

    multiply(waves[1], PIECES - 1)
    late = waves[1]

    def swap_late(col, sem):
        return pltpu.make_async_remote_copy(
            src_ref=acc.at[late, col],
            dst_ref=peer.at[late, col],
            send_sem=tail_send.at[sem],
            recv_sem=tail_recv.at[sem],
            device_id={"blk": sibling},
        )

    far = 2 * (1 - y)
    near_col = 2 * y + late
    swap_late(far + 1 - k, 2).start()

    @pl.when(k == y)
    def _():
        swap_late(far + k, 6).start()
        swap_late(near_col, 7).start()

    swap_late(far + k, 2).wait_recv()
    peer[late, far + k] += acc[late, far + k]
    turn_z(1)
    send_z(1).start()

    @pl.when(k != y)
    def _():
        swap_late(far + 1 - k, 6).wait_recv()
        peer[late, far + 1 - k] += acc[late, far + 1 - k]
        swap_late(near_col, 7).wait_recv()
        peer[late, near_col] += acc[late, near_col]
        send_y.start()
        turn_own(1)

    send_cross.wait_recv()
    out_ref[:, 2 * TILE : 3 * TILE] = diag[...]
    near = cross[...].T + crossrecv[...]
    send_y.wait_recv()

    @pl.when(k == y)
    def _():
        send_z(0).wait_recv()

    send_z(1).wait_recv()

    @pl.when(k == 0)
    def _():
        out_ref[:, 0:TILE] = ymsg[0] + lohi[0, 0]
        out_ref[:, TILE : 2 * TILE] = ymsg[1] + lohi[0, 1]
        out_ref[:, 3 * TILE : 4 * TILE] = near
        out_ref[:, 4 * TILE : 5 * TILE] = ymsg[2] + lohi[1, 0]

    @pl.when(k == 1)
    def _():
        out_ref[:, 0:TILE] = ymsg[0] + lohi[0, 1]
        out_ref[:, TILE : 2 * TILE] = near
        out_ref[:, 3 * TILE : 4 * TILE] = ymsg[1] + lohi[1, 0]
        out_ref[:, 4 * TILE : 5 * TILE] = ymsg[2] + lohi[1, 1]

    for core in range(2):
        for copy in (y_copy, z_copy):
            copy(core, 0, quarter, k, y_sem.at[k, 0]).wait_send()
    sib_one.wait_send()
    sib_two.wait_send()
    send_cross.wait_send()
    swap(0).wait_send()
    swap_late(far + 1 - k, 2).wait_send()

    @pl.when(k == y)
    def _():
        swap_late(far + k, 6).wait_send()
        swap_late(near_col, 7).wait_send()
        send_z(0).wait_send()

    send_y.wait_send()
    send_z(1).wait_send()


def body(n, half_blocks):
    columns = half_blocks.T
    depth, tile = columns.shape
    quarter = depth // 4
    band = pl.pallas_call(
        functools.partial(kernel, n),
        out_shape=jax.ShapeDtypeStruct((tile, 5 * tile), F32),
        in_specs=[pl.BlockSpec(memory_space=pl.ANY)],
        out_specs=pl.BlockSpec(memory_space=pltpu.VMEM),
        scratch_shapes=[
            pltpu.VMEM((depth, tile), jnp.bfloat16),
            pltpu.VMEM((4, quarter, tile), jnp.bfloat16),
            pltpu.VMEM((2, quarter, tile), jnp.bfloat16),
            pltpu.VMEM((quarter, tile), jnp.bfloat16),
            pltpu.VMEM((2, 4, tile, tile), F32),
            pltpu.VMEM((2, 4, tile, tile), F32),
            pltpu.VMEM((3, tile, tile), F32),
            pltpu.VMEM((2, 2, tile, tile), F32),
            pltpu.VMEM((2, tile, tile), F32),
            pltpu.VMEM((tile, tile), F32),
            pltpu.VMEM((tile, tile), F32),
            pltpu.VMEM((tile, tile), F32),
            pltpu.SemaphoreType.DMA((2,)),
            pltpu.SemaphoreType.DMA((6,)),
            pltpu.SemaphoreType.DMA((2, PIECES)),
            pltpu.SemaphoreType.DMA((2, PIECES)),
            pltpu.SemaphoreType.DMA((2,)),
            pltpu.SemaphoreType.DMA((8,)),
            pltpu.SemaphoreType.DMA((8,)),
        ],
        compiler_params=pltpu.CompilerParams(
            collective_id=0, has_side_effects=True, vmem_limit_bytes=50 * 1024 * 1024
        ),
    )(columns)
    return band * (1.0 / math.sqrt(depth))


def solution(mesh):
    return jax.shard_map(
        functools.partial(body, mesh.shape["blk"]),
        mesh=mesh,
        in_specs=(P(("parts", "blk"), None),),
        out_specs=P(("parts", "blk"), None),
        check_vma=False,
    )
```
